512 devices in a mesh: dp: 16 (over y_hi, x, core), tensor: 32 (over z, y_lo).
Axes of the slice: x: 4, y: 8 (y_hi: 2, y_lo: 4; y = y_hi * 4 + y_lo), z: 8, core: 2. Of those that a mesh axis runs over, the one named last changes fastest.
Arguments:
- drafts: bfloat16 [768, 8192], P('tensor', 'dp'), may hold values from -6 to 6
- gate_codes: bfloat16 [8192, 28672], P('dp', 'tensor'), may hold values from -8 to 7, as said below
- gate_scales: float32 [64, 28672], P('dp', 'tensor'), may hold values from 0.0012 to 0.0048
- up_codes: bfloat16 [8192, 28672], P('dp', 'tensor'), may hold values from -8 to 7, as said below
- up_scales: float32 [64, 28672], P('dp', 'tensor'), may hold values from 0.0012 to 0.0048
- down_codes: bfloat16 [28672, 8192], P('tensor', 'dp'), may hold values from -8 to 7, as said below
- down_scales: float32 [224, 8192], P('tensor', 'dp'), may hold values from 0.0006 to 0.0024
Outputs:
- layer_out: bfloat16 [768, 8192], P('tensor', 'dp')
The draws below stay inside these ranges and needn't reach their ends.
Inputs may be any that keep to these rules, and one draw needn't show every extreme that they name: `gate_codes`: every code is an integer. `up_codes`: every code is an integer. `down_codes`: every code is an integer.
All inputs are finite; a program needn't handle non-finite values.
Results may differ from the reference program's by a relative error of at most 0.04.
Values may be sent and summed in bfloat16 or wider, within the bound.
No kernel may reach another device: no remote copies, remote signals or barrier semaphores. Data moves between devices by JAX's collectives and lax.ppermute only.
A program may use at most 64 MiB of HBM per device.

```python
import math
import jax
import jax.numpy as jnp
import numpy as np
from jax import lax

D = 8192
HK = 28
HB = 1024
G = 128
FF = 28672
ROWS = 768
N_DP = 16
N_TENSOR = 32


def draw_gate_codes(key, part):
    key = jax.random.fold_in(key, 11)
    return jax.random.randint(key, (D, FF), -8, 8).astype(jnp.float32).astype(jnp.bfloat16)


def draw_up_codes(key, part):
    key = jax.random.fold_in(key, 23)
    return jax.random.randint(key, (D, FF), -8, 8).astype(jnp.float32).astype(jnp.bfloat16)


def draw_down_codes(key, part):
    key = jax.random.fold_in(key, 37)
    return jax.random.randint(key, (FF, D), -8, 8).astype(jnp.float32).astype(jnp.bfloat16)


def strengthened(entries, key, source, target, blocks, factor):
    owner, partner = [(jnp.arange(entries.shape[axis_at]) // (entries.shape[axis_at] // blocks)).reshape([-1 if axis == axis_at else 1 for axis in range(entries.ndim)]) for axis_at in (source, target)]
    chosen = jax.random.permutation(key, blocks)[partner]
    strong = (owner == chosen) | (owner == (partner + blocks // 2) % blocks)
    return jnp.where(strong, factor * entries, entries)


def block_scale(stream_key, shape, pieces, low, top_value):
    def one(position, shards_of):
        steps = jax.random.uniform(jax.random.fold_in(jax.random.fold_in(stream_key, 6), position), (shards_of,), jnp.float32, low / len(pieces), top_value / len(pieces))
        return jnp.repeat(jnp.exp(steps), shape[position] // shards_of).reshape((-1,) + (1,) * (len(shape) - position - 1))

    gain = one(*pieces[0])
    for cut in pieces[1:]:
        gain = gain * one(*cut)
    return gain


def noise_with(own_key, shape, width, reach, cuts, heavy, kind=jnp.bfloat16):
    drawn = width * jax.random.normal(own_key, shape, jnp.float32)
    if cuts:
        drawn = drawn * block_scale(own_key, shape, cuts, -0.22, 0.18)
    return jnp.clip(strengthened(drawn, jax.random.fold_in(own_key, 3), *heavy), -reach, reach).astype(kind)


def setup_inputs(seed: int = 0) -> dict:
    key_of = jax.random.split(jax.random.key(seed), 8)
    return {
        "drafts": noise_with(key_of[0], (ROWS, D), 1.0, 6.0, ((0, 32), (1, 16)), (1, 0, 32, 2.75)),
        "gate_codes": draw_gate_codes(jax.random.fold_in(key_of[7], 71), 0),
        "gate_scales": jnp.clip(jnp.exp(math.log(0.0048) - 1.3862944 * jax.random.uniform(key_of[2], (D // G, FF), jnp.float32) ** block_scale(key_of[2], (D // G, FF), ((0, 16), (1, 32)), -0.2, 0.2)), 0.0012, 0.0048),
        "up_codes": draw_up_codes(jax.random.fold_in(key_of[7], 71), 0),
        "up_scales": jnp.clip(jnp.exp(math.log(0.0048) - 1.3862944 * jax.random.uniform(key_of[4], (D // G, FF), jnp.float32) ** block_scale(key_of[4], (D // G, FF), ((0, 16), (1, 32)), -0.2, 0.2)), 0.0012, 0.0048),
        "down_codes": draw_down_codes(jax.random.fold_in(key_of[7], 71), 0),
        "down_scales": jnp.clip(jnp.exp(math.log(0.0024) - 1.3862944 * jax.random.uniform(key_of[6], (FF // G, D), jnp.float32) ** block_scale(key_of[6], (FF // G, D), ((0, 32), (1, 16)), -0.2, 0.2)), 0.0006, 0.0024),
    }


def paley_matrix():
    modulus = 13
    residues = set((number * number % modulus for number in range(1, modulus)))
    character = np.array([0] + [1 if number in residues else -1 for number in range(1, modulus)])
    jacobsthal = character[(np.arange(modulus)[:, None] - np.arange(modulus)[None, :]) % modulus]
    top_row = np.concatenate([np.zeros((1, 1)), np.ones((1, modulus))], axis=1)
    lower_rows = np.concatenate([np.ones((modulus, 1)), jacobsthal], axis=1)
    conference = np.concatenate([top_row, lower_rows], axis=0)
    first_part = np.kron(conference, np.array([[1.0, -1.0], [-1.0, -1.0]]))
    second_part = np.kron(np.eye(modulus + 1), np.array([[1.0, 1.0], [1.0, -1.0]]))
    return jnp.asarray(first_part + second_part, dtype=jnp.float32)

def walsh(extent):
    indices = jnp.arange(extent, dtype=jnp.int32)
    common = jnp.bitwise_and(indices[:, None], indices[None, :])
    parity = jnp.zeros((extent, extent), jnp.int32)
    for bit_pos in range(max(extent.bit_length() - 1, 0)):
        parity = parity + jnp.bitwise_and(jnp.right_shift(common, bit_pos), 1)
    return (1 - 2 * jnp.bitwise_and(parity, 1)).astype(jnp.float32)

def dequantize(codes, scales, group):
    row_count, col_count = codes.shape
    grouped = codes.astype(jnp.float32).reshape(row_count // group, group, col_count) * scales[:, None, :]
    return grouped.reshape(row_count, col_count).astype(jnp.bfloat16)

def rounded(values):
    return lax.optimization_barrier(values.astype(jnp.bfloat16)).astype(jnp.float32)

def reference(drafts, gate_codes, gate_scales, up_codes, up_scales, down_codes, down_scales):
    in_block = D // N_DP

    def gate_step(block_id, totals):
        start = (block_id * in_block).astype(jnp.int32)
        group_start = (block_id * (in_block // G)).astype(jnp.int32)
        rows_part = lax.dynamic_slice_in_dim(drafts, start, in_block, 1)
        gate_w = dequantize(lax.dynamic_slice_in_dim(gate_codes, start, in_block, 0), lax.dynamic_slice_in_dim(gate_scales, group_start, in_block // G, 0), G)
        up_w = dequantize(lax.dynamic_slice_in_dim(up_codes, start, in_block, 0), lax.dynamic_slice_in_dim(up_scales, group_start, in_block // G, 0), G)
        gate_part = rounded(jnp.dot(rows_part, gate_w, preferred_element_type=jnp.float32))
        up_part = rounded(jnp.dot(rows_part, up_w, preferred_element_type=jnp.float32))
        return (totals[0] + gate_part, totals[1] + up_part)
    empty = jnp.zeros((ROWS, FF), jnp.float32)
    gate, up = lax.fori_loop(0, N_DP, gate_step, (empty, empty))
    hidden = (jax.nn.silu(gate) * up).astype(jnp.bfloat16)
    spread = hidden.astype(jnp.float32).reshape(ROWS, HB, HK)
    spread = jnp.einsum('rjk,ik->rji', spread, paley_matrix(), precision=lax.Precision.HIGHEST)
    spread = jnp.einsum('mj,rji->rmi', walsh(HB), spread, precision=lax.Precision.HIGHEST)
    rotated = (spread * (1.0 / math.sqrt(HK * HB))).reshape(ROWS, FF).astype(jnp.bfloat16)
    out_block = FF // N_TENSOR

    def down_step(block_id, total):
        start = (block_id * out_block).astype(jnp.int32)
        group_start = (block_id * (out_block // G)).astype(jnp.int32)
        piece = lax.dynamic_slice_in_dim(rotated, start, out_block, 1)
        down_w = dequantize(lax.dynamic_slice_in_dim(down_codes, start, out_block, 0), lax.dynamic_slice_in_dim(down_scales, group_start, out_block // G, 0), G)
        return total + rounded(jnp.dot(piece, down_w, preferred_element_type=jnp.float32))
    layer_out = lax.fori_loop(0, N_TENSOR, down_step, jnp.zeros((ROWS, D), jnp.float32))
    return layer_out.astype(jnp.bfloat16)
```

```python
import math

import jax
import jax.numpy as jnp
import ml_dtypes
import numpy as np
from jax import lax
from jax.experimental import pallas as pl
from jax.experimental.pallas import tpu as pltpu
from jax.sharding import Mesh
from jax.sharding import PartitionSpec as P

HK = 28
HB = 1024
G = 128
N_T = 32
SPAN = HB // N_T
UNITS = SPAN * HK
GROUP = 56
GROUPS = UNITS // GROUP
LANES = 128
CORES = [(0, 1), (1, 0)]
SCALE = 1.0 / math.sqrt(HK * HB)


def paley_matrix():
    modulus = 13
    residues = set((number * number % modulus for number in range(1, modulus)))
    character = np.array([0] + [1 if number in residues else -1 for number in range(1, modulus)])
    jacobsthal = character[(np.arange(modulus)[:, None] - np.arange(modulus)[None, :]) % modulus]
    top_row = np.concatenate([np.zeros((1, 1)), np.ones((1, modulus))], axis=1)
    lower_rows = np.concatenate([np.ones((modulus, 1)), jacobsthal], axis=1)
    conference = np.concatenate([top_row, lower_rows], axis=0)
    first_part = np.kron(conference, np.array([[1.0, -1.0], [-1.0, -1.0]]))
    second_part = np.kron(np.eye(modulus + 1), np.array([[1.0, 1.0], [1.0, -1.0]]))
    return first_part + second_part


def walsh(extent):
    matrix = np.ones((1, 1))
    while matrix.shape[0] < extent:
        matrix = np.kron(np.array([[1.0, 1.0], [1.0, -1.0]]), matrix)
    return matrix


def block_matrix():
    return np.kron(walsh(SPAN), paley_matrix()).T.astype(ml_dtypes.bfloat16)


def dequantize(codes, scales):
    row_count, col_count = codes.shape
    grouped = (
        codes.astype(jnp.float32).reshape(row_count // G, G, col_count) * scales[:, None, :]
    )
    return grouped.reshape(row_count, col_count).astype(jnp.bfloat16)


def whole(memory=pltpu.VMEM):
    return pl.BlockSpec(memory_space=memory)


def call(kernel, out_shape, operands, flops, name):
    return pl.pallas_call(
        kernel,
        out_shape=jax.ShapeDtypeStruct(out_shape, jnp.bfloat16),
        in_specs=[whole()] * len(operands),
        out_specs=whole(),
        name=name,
        compiler_params=pltpu.CompilerParams(vmem_limit_bytes=32 * 1024 * 1024),
        cost_estimate=pl.CostEstimate(flops=flops, bytes_accessed=2_000_000, transcendentals=0),
    )(*operands)


def sum_and_cut(parts_ref, out_ref):
    total = parts_ref[0].astype(jnp.float32)
    for part in range(1, parts_ref.shape[0]):
        total = total + parts_ref[part].astype(jnp.float32)
    for group in range(GROUPS):
        start = 2 * GROUP * group
        tile, offset = start // LANES, start % LANES
        piece = total[:, tile * LANES : (tile + 1) * LANES]
        if offset:
            piece = pltpu.roll(piece, LANES - offset, 1)
            if offset + 2 * GROUP > LANES:
                after = total[:, (tile + 1) * LANES : (tile + 2) * LANES]
                after = pltpu.roll(after, LANES - offset, 1)
                lane = lax.broadcasted_iota(jnp.int32, piece.shape, 1)
                piece = jnp.where(lane < LANES - offset, piece, after)
        piece = piece.astype(jnp.bfloat16)
        for rows in range(4):
            out_ref[rows * GROUPS + group] = piece[rows * 24 : rows * 24 + 24]


def gate_and_mix(sums_ref, out_ref):
    sums = sums_ref[0].astype(jnp.float32) + sums_ref[1].astype(jnp.float32)
    lane = lax.broadcasted_iota(jnp.int32, (N_T, 8, LANES), 2)
    packed = []
    for tile in range(3):
        gate = sums[:, tile * 8 : tile * 8 + 8]
        up = pltpu.roll(gate, LANES - GROUP, 2)
        value = (gate / (1.0 + jnp.exp(-gate)) * up).astype(jnp.bfloat16).astype(jnp.float32)
        value = jnp.where(lane < GROUP, value, 0.0)
        half = 1
        while half < N_T:
            split = value.reshape(N_T // (2 * half), 2, half, 8, LANES)
            low, high = split[:, 0], split[:, 1]
            value = jnp.stack([low + high, low - high], axis=1).reshape(N_T, 8, LANES)
            half *= 2
        packed.append(value * SCALE)
    first = jnp.where(lane < GROUP, packed[0], pltpu.roll(packed[1], GROUP, 2))
    both = jnp.concatenate([first, packed[2]], axis=1).astype(jnp.bfloat16)
    out_ref[0] = both
    out_ref[1] = both


def join_and_mix(pieces_ref, matrix_ref, out_ref):
    lane = lax.broadcasted_iota(jnp.int32, (8, LANES), 1)
    rows = []
    for block in range(4):
        tiles = [[None] * (UNITS // LANES) for _ in range(3)]
        for group in range(GROUPS):
            piece = pieces_ref[block * GROUPS + group].astype(jnp.float32)
            start = GROUP * group
            tile, offset = start // LANES, start % LANES
            for row, (source, shift) in enumerate(((0, 0), (0, GROUP), (1, 0))):
                moved = piece[source * 8 : source * 8 + 8]
                turn = (offset - shift) % LANES
                if turn:
                    moved = pltpu.roll(moved, turn, 1)
                line = tiles[row]
                line[tile] = moved if line[tile] is None else jnp.where(lane < offset, line[tile], moved)
                if offset + GROUP > LANES:
                    line[tile + 1] = moved
        rows += [jnp.concatenate(line, axis=1) for line in tiles]
    units = jnp.concatenate(rows, axis=0).astype(jnp.bfloat16)
    mixed = jnp.dot(units, matrix_ref[...], preferred_element_type=jnp.float32).astype(jnp.bfloat16)
    for copy in range(out_ref.shape[0]):
        out_ref[copy] = mixed


def per_device(drafts, gate_codes, gate_scales, up_codes, up_scales, down_codes, down_scales):
    core = lax.axis_index("c")
    depth = drafts.shape[1]
    rows = drafts.shape[0] * N_T
    half = rows // 2
    gathered = lax.all_to_all(
        jnp.broadcast_to(drafts[None], (N_T,) + drafts.shape), ("z", "yl"), 0, 0, tiled=True
    ).reshape(rows, depth)
    both_weights = jnp.concatenate(
        [
            dequantize(gate_codes, gate_scales).reshape(depth, GROUPS, GROUP),
            dequantize(up_codes, up_scales).reshape(depth, GROUPS, GROUP),
        ],
        axis=2,
    ).reshape(depth, 2 * UNITS)
    theirs = lax.dynamic_slice_in_dim(gathered, (1 - core) * half, half, 0)
    ours = lax.dynamic_slice_in_dim(gathered, core * half, half, 0)
    sent = jnp.dot(theirs, both_weights, preferred_element_type=jnp.float32).astype(jnp.bfloat16)
    received = lax.ppermute(sent, "c", CORES)
    kept = jnp.dot(ours, both_weights, preferred_element_type=jnp.float32)
    sums = (kept + received.astype(jnp.float32)).astype(jnp.bfloat16)
    sums = lax.all_to_all(sums.reshape(4, half // 4, 2 * UNITS), "x", 0, 0, tiled=True)
    pieces = call(sum_and_cut, (4 * GROUPS, 24, LANES), (sums,), 1_000_000, "sum_and_cut")
    pieces = lax.all_to_all(pieces, ("yh", "z", "yl"), 0, 0, tiled=True)
    pieces = call(
        gate_and_mix, (2, N_T, 16, LANES), (pieces.reshape(2, N_T, 24, LANES),), 2_000_000, "gate_and_mix"
    )
    pieces = lax.all_to_all(pieces.reshape(2 * N_T, 16, LANES), ("yh", "z", "yl"), 0, 0, tiled=True)
    rotated = call(
        join_and_mix,
        (4, half // 4, UNITS),
        (pieces, jnp.asarray(block_matrix())),
        200_000_000,
        "join_and_mix",
    )
    rotated = lax.all_to_all(rotated, "x", 0, 0, tiled=True).reshape(half, UNITS)
    other = lax.ppermute(rotated, "c", CORES)
    down_weights = dequantize(down_codes, down_scales)
    own_part = jnp.dot(rotated, down_weights, preferred_element_type=jnp.float32)
    other_part = jnp.dot(other, down_weights, preferred_element_type=jnp.float32)
    own_part, other_part = own_part.astype(jnp.bfloat16), other_part.astype(jnp.bfloat16)
    partial_value = jnp.zeros((rows, own_part.shape[1]), jnp.bfloat16)
    partial_value = lax.dynamic_update_slice_in_dim(partial_value, own_part, core * half, 0)
    partial_value = lax.dynamic_update_slice_in_dim(partial_value, other_part, (1 - core) * half, 0)
    partial_value = lax.all_to_all(
        partial_value.reshape(N_T, rows // N_T, own_part.shape[1]), ("z", "yl"), 0, 0, tiled=True
    )
    return jnp.sum(partial_value.astype(jnp.float32), axis=0).astype(jnp.bfloat16)


def solution(mesh):
    fine = Mesh(mesh.devices.reshape(2, 4, 2, 8, 4), ("yh", "x", "c", "z", "yl"))
    dp, tensor = ("yh", "x", "c"), ("z", "yl")
    return jax.shard_map(
        per_device,
        mesh=fine,
        in_specs=(
            P(tensor, dp),
            P(dp, tensor),
            P(dp, tensor),
            P(dp, tensor),
            P(dp, tensor),
            P(tensor, dp),
            P(tensor, dp),
        ),
        out_specs=P(tensor, dp),
        check_vma=False,
    )
```

```python
import functools
import math

import jax
import jax.numpy as jnp
import ml_dtypes
import numpy as np
from jax import lax
from jax.experimental import pallas as pl
from jax.experimental.pallas import tpu as pltpu
from jax.sharding import Mesh
from jax.sharding import PartitionSpec as P

HK = 28
HB = 1024
G = 128
N_T = 32
SPAN = HB // N_T
UNITS = SPAN * HK
GROUP = 56
GROUPS = UNITS // GROUP
LANES = 128
CORES = [(0, 1), (1, 0)]
SCALE = 1.0 / math.sqrt(HK * HB)


def paley_matrix():
    modulus = 13
    residues = set((number * number % modulus for number in range(1, modulus)))
    character = np.array([0] + [1 if number in residues else -1 for number in range(1, modulus)])
    jacobsthal = character[(np.arange(modulus)[:, None] - np.arange(modulus)[None, :]) % modulus]
    top_row = np.concatenate([np.zeros((1, 1)), np.ones((1, modulus))], axis=1)
    lower_rows = np.concatenate([np.ones((modulus, 1)), jacobsthal], axis=1)
    conference = np.concatenate([top_row, lower_rows], axis=0)
    first_part = np.kron(conference, np.array([[1.0, -1.0], [-1.0, -1.0]]))
    second_part = np.kron(np.eye(modulus + 1), np.array([[1.0, 1.0], [1.0, -1.0]]))
    return first_part + second_part


def walsh(extent):
    matrix = np.ones((1, 1))
    while matrix.shape[0] < extent:
        matrix = np.kron(np.array([[1.0, 1.0], [1.0, -1.0]]), matrix)
    return matrix


def block_matrix():
    return np.kron(walsh(SPAN), paley_matrix()).T.astype(ml_dtypes.bfloat16)


def dequantize(codes, scales):
    row_count, col_count = codes.shape
    grouped = (
        codes.astype(jnp.float32).reshape(row_count // G, G, col_count) * scales[:, None, :]
    )
    return grouped.reshape(row_count, col_count).astype(jnp.bfloat16)


def whole(memory=pltpu.VMEM):
    return pl.BlockSpec(memory_space=memory)


def call(kernel, name, out_shape, operands, flops, dtype=jnp.bfloat16, memory=pltpu.VMEM, scratch=()):
    return pl.pallas_call(
        kernel,
        out_shape=jax.ShapeDtypeStruct(out_shape, dtype),
        in_specs=[whole()] * len(operands),
        out_specs=whole(memory),
        scratch_shapes=list(scratch),
        name=name,
        compiler_params=pltpu.CompilerParams(vmem_limit_bytes=32 * 1024 * 1024),
        cost_estimate=pl.CostEstimate(flops=flops, bytes_accessed=2_000_000, transcendentals=0),
    )(*operands)


def copy_out(block_ref, out_ref, held, sems):
    at_once = held.shape[0]
    for index in range(at_once):
        held[index] = block_ref[...]
    copies = [
        pltpu.make_async_copy(held, out_ref.at[pl.ds(at_once * index, at_once)], sems.at[index])
        for index in range(out_ref.shape[0] // at_once)
    ]
    for copy in copies:
        copy.start()
    for copy in copies:
        copy.wait()


def rows_times(flip, rows_ref, weights_ref, out_ref):
    half = out_ref.shape[0]
    core = lax.axis_index("c")
    mine = 1 - core if flip else core
    rows = rows_ref[pl.ds(pl.multiple_of(mine * half, half), half), :]
    out_ref[...] = jnp.dot(rows, weights_ref[...], preferred_element_type=jnp.float32).astype(out_ref.dtype)


def add_parts(kept_ref, received_ref, out_ref, held, sems):
    blocks, size = out_ref.shape[0], out_ref.shape[1]
    copies = []
    for block in range(blocks):
        rows = pl.ds(block * size, size)
        held[block] = (kept_ref[rows, :] + received_ref[rows, :].astype(jnp.float32)).astype(jnp.bfloat16)
        copies.append(pltpu.make_async_copy(held.at[block], out_ref.at[block], sems.at[block]))
        copies[-1].start()
    for copy in copies:
        copy.wait()


def sum_and_cut(parts_ref, out_ref):
    total = parts_ref[0].astype(jnp.float32)
    for part in range(1, parts_ref.shape[0]):
        total = total + parts_ref[part].astype(jnp.float32)
    for group in range(GROUPS):
        start = 2 * GROUP * group
        tile, offset = start // LANES, start % LANES
        piece = total[:, tile * LANES : (tile + 1) * LANES]
        if offset:
            piece = pltpu.roll(piece, LANES - offset, 1)
            if offset + 2 * GROUP > LANES:
                after = total[:, (tile + 1) * LANES : (tile + 2) * LANES]
                after = pltpu.roll(after, LANES - offset, 1)
                lane = lax.broadcasted_iota(jnp.int32, piece.shape, 1)
                piece = jnp.where(lane < LANES - offset, piece, after)
        piece = piece.astype(jnp.bfloat16)
        for rows in range(4):
            out_ref[rows * GROUPS + group] = piece[rows * 24 : rows * 24 + 24]


def gate_and_mix(sums_ref, out_ref):
    sums = sums_ref[:, 0].astype(jnp.float32) + sums_ref[:, 1].astype(jnp.float32)
    lane = lax.broadcasted_iota(jnp.int32, (N_T, 8, LANES), 2)
    packed = []
    for tile in range(3):
        gate = sums[:, tile * 8 : tile * 8 + 8]
        up = pltpu.roll(gate, LANES - GROUP, 2)
        value = (gate / (1.0 + jnp.exp(-gate)) * up).astype(jnp.bfloat16).astype(jnp.float32)
        value = jnp.where(lane < GROUP, value, 0.0)
        half = 1
        while half < N_T:
            split = value.reshape(N_T // (2 * half), 2, half, 8, LANES)
            low, high = split[:, 0], split[:, 1]
            value = jnp.stack([low + high, low - high], axis=1).reshape(N_T, 8, LANES)
            half *= 2
        packed.append(value * SCALE)
    first = jnp.where(lane < GROUP, packed[0], pltpu.roll(packed[1], GROUP, 2))
    both = jnp.concatenate([first, packed[2]], axis=1).astype(jnp.bfloat16)
    out_ref[:, 0] = both
    out_ref[:, 1] = both


def join_and_mix(pieces_ref, matrix_ref, out_ref):
    lane = lax.broadcasted_iota(jnp.int32, (8, LANES), 1)
    rows = []
    for block in range(4):
        tiles = [[None] * (UNITS // LANES) for _ in range(3)]
        for group in range(GROUPS):
            piece = pieces_ref[block * GROUPS + group].astype(jnp.float32)
            start = GROUP * group
            tile, offset = start // LANES, start % LANES
            for row, (source, shift) in enumerate(((0, 0), (0, GROUP), (1, 0))):
                moved = piece[source * 8 : source * 8 + 8]
                turn = (offset - shift) % LANES
                if turn:
                    moved = pltpu.roll(moved, turn, 1)
                line = tiles[row]
                line[tile] = moved if line[tile] is None else jnp.where(lane < offset, line[tile], moved)
                if offset + GROUP > LANES:
                    line[tile + 1] = moved
        rows += [jnp.concatenate(line, axis=1) for line in tiles]
    units = jnp.concatenate(rows, axis=0).astype(jnp.bfloat16)
    mixed = jnp.dot(units, matrix_ref[...], preferred_element_type=jnp.float32).astype(jnp.bfloat16)
    for copy in range(out_ref.shape[0]):
        out_ref[copy] = mixed


def per_device(drafts, gate_codes, gate_scales, up_codes, up_scales, down_codes, down_scales):
    core = lax.axis_index("c")
    depth = drafts.shape[1]
    rows = drafts.shape[0] * N_T
    half = rows // 2
    everyone = ("z", "yl", "yh")
    copies = call(
        copy_out,
        "copy_out",
        (N_T,) + drafts.shape,
        (drafts,),
        1_000,
        memory=pltpu.HBM,
        scratch=[pltpu.VMEM((8,) + drafts.shape, drafts.dtype), pltpu.SemaphoreType.DMA((N_T // 8,))],
    )
    gathered = lax.all_to_all(copies, ("z", "yl"), 0, 0, tiled=True).reshape(rows, depth)
    both_weights = jnp.concatenate(
        [
            dequantize(gate_codes, gate_scales).reshape(depth, GROUPS, GROUP),
            dequantize(up_codes, up_scales).reshape(depth, GROUPS, GROUP),
        ],
        axis=2,
    ).reshape(depth, 2 * UNITS)
    flops = rows * depth * 2 * UNITS
    sent = call(
        functools.partial(rows_times, True), "their_rows", (half, 2 * UNITS), (gathered, both_weights), flops
    )
    received = lax.ppermute(sent, "c", CORES)
    kept = call(
        functools.partial(rows_times, False),
        "our_rows",
        (half, 2 * UNITS),
        (gathered, both_weights),
        flops,
        dtype=jnp.float32,
    )
    sums = call(
        add_parts,
        "add_parts",
        (4, half // 4, 2 * UNITS),
        (kept, received),
        1_000_000,
        memory=pltpu.HBM,
        scratch=[pltpu.VMEM((4, half // 4, 2 * UNITS), jnp.bfloat16), pltpu.SemaphoreType.DMA((4,))],
    )
    sums = lax.all_to_all(sums, "x", 0, 0, tiled=True)
    pieces = call(sum_and_cut, "sum_and_cut", (4 * GROUPS, 24, LANES), (sums,), 1_000_000)
    pieces = lax.all_to_all(pieces, everyone, 0, 0, tiled=True)
    pieces = call(
        gate_and_mix, "gate_and_mix", (N_T, 2, 16, LANES), (pieces.reshape(N_T, 2, 24, LANES),), 2_000_000
    )
    pieces = lax.all_to_all(pieces.reshape(2 * N_T, 16, LANES), everyone, 0, 0, tiled=True)
    rotated = call(
        join_and_mix, "join_and_mix", (4, half // 4, UNITS), (pieces, jnp.asarray(block_matrix())), 200_000_000
    )
    rotated = lax.all_to_all(rotated, "x", 0, 0, tiled=True).reshape(half, UNITS)
    other = lax.ppermute(rotated, "c", CORES)
    down_weights = dequantize(down_codes, down_scales)
    own_part = jnp.dot(rotated, down_weights, preferred_element_type=jnp.float32)
    other_part = jnp.dot(other, down_weights, preferred_element_type=jnp.float32)
    own_part, other_part = own_part.astype(jnp.bfloat16), other_part.astype(jnp.bfloat16)
    partial_value = jnp.zeros((rows, own_part.shape[1]), jnp.bfloat16)
    partial_value = lax.dynamic_update_slice_in_dim(partial_value, own_part, core * half, 0)
    partial_value = lax.dynamic_update_slice_in_dim(partial_value, other_part, (1 - core) * half, 0)
    partial_value = lax.all_to_all(
        partial_value.reshape(N_T, rows // N_T, own_part.shape[1]), ("z", "yl"), 0, 0, tiled=True
    )
    return jnp.sum(partial_value.astype(jnp.float32), axis=0).astype(jnp.bfloat16)


def solution(mesh):
    fine = Mesh(mesh.devices.reshape(2, 4, 2, 8, 4), ("yh", "x", "c", "z", "yl"))
    dp, tensor = ("yh", "x", "c"), ("z", "yl")
    return jax.shard_map(
        per_device,
        mesh=fine,
        in_specs=(
            P(tensor, dp),
            P(dp, tensor),
            P(dp, tensor),
            P(dp, tensor),
            P(dp, tensor),
            P(tensor, dp),
            P(tensor, dp),
        ),
        out_specs=P(tensor, dp),
        check_vma=False,
    )
```

```python
import functools
import math

import jax
import jax.numpy as jnp
import ml_dtypes
import numpy as np
from jax import lax
from jax.experimental import pallas as pl
from jax.experimental.pallas import tpu as pltpu
from jax.sharding import Mesh
from jax.sharding import PartitionSpec as P

HK = 28
HB = 1024
G = 128
N_T = 32
SPAN = HB // N_T
UNITS = SPAN * HK
GROUP = 56
GROUPS = UNITS // GROUP
LANES = 128
CORES = [(0, 1), (1, 0)]
SCALE = 1.0 / math.sqrt(HK * HB)


def paley_matrix():
    modulus = 13
    residues = set((number * number % modulus for number in range(1, modulus)))
    character = np.array([0] + [1 if number in residues else -1 for number in range(1, modulus)])
    jacobsthal = character[(np.arange(modulus)[:, None] - np.arange(modulus)[None, :]) % modulus]
    top_row = np.concatenate([np.zeros((1, 1)), np.ones((1, modulus))], axis=1)
    lower_rows = np.concatenate([np.ones((modulus, 1)), jacobsthal], axis=1)
    conference = np.concatenate([top_row, lower_rows], axis=0)
    first_part = np.kron(conference, np.array([[1.0, -1.0], [-1.0, -1.0]]))
    second_part = np.kron(np.eye(modulus + 1), np.array([[1.0, 1.0], [1.0, -1.0]]))
    return first_part + second_part


def walsh(extent):
    matrix = np.ones((1, 1))
    while matrix.shape[0] < extent:
        matrix = np.kron(np.array([[1.0, 1.0], [1.0, -1.0]]), matrix)
    return matrix


def block_matrix():
    return np.kron(walsh(SPAN), paley_matrix()).T.astype(ml_dtypes.bfloat16)


def dequantize(codes, scales):
    row_count, col_count = codes.shape
    grouped = (
        codes.astype(jnp.float32).reshape(row_count // G, G, col_count) * scales[:, None, :]
    )
    return grouped.reshape(row_count, col_count).astype(jnp.bfloat16)


def whole(memory=pltpu.VMEM):
    return pl.BlockSpec(memory_space=memory)


def call(kernel, name, out_shape, operands, flops, memory=pltpu.VMEM, scratch=(), specs=None):
    places = specs or [pltpu.VMEM] * len(operands)
    if isinstance(out_shape, list):
        shapes = [jax.ShapeDtypeStruct(shape, dtype) for shape, dtype in out_shape]
        results = [whole(memory)] * len(shapes)
    else:
        shapes, results = jax.ShapeDtypeStruct(out_shape, jnp.bfloat16), whole(memory)
    return pl.pallas_call(
        kernel,
        out_shape=shapes,
        in_specs=[whole(place) for place in places],
        out_specs=results,
        scratch_shapes=list(scratch),
        name=name,
        compiler_params=pltpu.CompilerParams(vmem_limit_bytes=32 * 1024 * 1024),
        cost_estimate=pl.CostEstimate(flops=flops, bytes_accessed=2_000_000, transcendentals=0),
    )(*operands)


def copy_out(block_ref, out_ref, held, sems):
    at_once = held.shape[0]
    for index in range(at_once):
        held[index] = block_ref[...]
    copies = [
        pltpu.make_async_copy(held, out_ref.at[pl.ds(at_once * index, at_once)], sems.at[index])
        for index in range(out_ref.shape[0] // at_once)
    ]
    for copy in copies:
        copy.start()
    for copy in copies:
        copy.wait()


def dequantize_pair(gate_ref, gate_scales_ref, up_ref, up_scales_ref, out_ref):
    for group in range(gate_scales_ref.shape[0]):
        rows = pl.ds(group * G, G)
        line = slice(group, group + 1)
        gate = gate_ref[rows, :].astype(jnp.float32) * gate_scales_ref[line, :]
        up = up_ref[rows, :].astype(jnp.float32) * up_scales_ref[line, :]
        out_ref[rows, :UNITS] = gate.astype(jnp.bfloat16)
        out_ref[rows, UNITS:] = up.astype(jnp.bfloat16)


def take_theirs(rows_ref, out_ref):
    half = out_ref.shape[0]
    start = (1 - lax.axis_index("c")) * half
    out_ref[...] = rows_ref[pl.ds(pl.multiple_of(start, half), half), :]


def times_own(after_ref, rows_ref, weights_ref, other_ref, out_ref, held_ref, sems):
    step = other_ref.shape[0] // sems.shape[0]
    copies = []
    for index in range(sems.shape[0]):
        lines = pl.ds(index * step, step)
        copies.append(pltpu.make_async_copy(other_ref.at[lines], held_ref.at[lines], sems.at[index]))
        copies[-1].start()
    half = out_ref.shape[0]
    start = lax.axis_index("c") * half
    rows = rows_ref[pl.ds(pl.multiple_of(start, half), half), :]
    out_ref[...] = jnp.dot(rows, weights_ref[...], preferred_element_type=jnp.float32)
    for copy in copies:
        copy.wait()


def add_other(part_ref, rows_ref, weights_ref, out_ref):
    total = part_ref[...] + jnp.dot(rows_ref[...], weights_ref[...], preferred_element_type=jnp.float32)
    out_ref[...] = total.astype(jnp.bfloat16)


def sum_and_cut(parts_ref, out_ref):
    total = parts_ref[0].astype(jnp.float32)
    for part in range(1, parts_ref.shape[0]):
        total = total + parts_ref[part].astype(jnp.float32)
    lane = lax.broadcasted_iota(jnp.int32, (total.shape[0], LANES), 1)
    for group in range(GROUPS):
        offset = GROUP * group % LANES
        halves = []
        for base, shift in ((0, 0), (UNITS, GROUP)):
            tile = (base + GROUP * group) // LANES * LANES
            piece = total[:, tile : tile + LANES]
            if offset + GROUP > LANES:
                piece = jnp.where(lane < offset, total[:, tile + LANES : tile + 2 * LANES], piece)
            turn = (shift - offset) % LANES
            halves.append(pltpu.roll(piece, turn, 1) if turn else piece)
        piece = jnp.where(lane < GROUP, halves[0], halves[1]).astype(jnp.bfloat16)
        for rows in range(4):
            out_ref[rows * GROUPS + group] = piece[rows * 24 : rows * 24 + 24]


def gate_and_mix(sums_ref, out_ref):
    sums = sums_ref[:, 0].astype(jnp.float32) + sums_ref[:, 1].astype(jnp.float32)
    lane = lax.broadcasted_iota(jnp.int32, (N_T, 8, LANES), 2)
    packed = []
    for tile in range(3):
        gate = sums[:, tile * 8 : tile * 8 + 8]
        up = pltpu.roll(gate, LANES - GROUP, 2)
        value = (gate / (1.0 + jnp.exp(-gate)) * up).astype(jnp.bfloat16).astype(jnp.float32)
        value = jnp.where(lane < GROUP, value, 0.0)
        half = 1
        while half < N_T:
            split = value.reshape(N_T // (2 * half), 2, half, 8, LANES)
            low, high = split[:, 0], split[:, 1]
            value = jnp.stack([low + high, low - high], axis=1).reshape(N_T, 8, LANES)
            half *= 2
        packed.append(value * SCALE)
    first = jnp.where(lane < GROUP, packed[0], pltpu.roll(packed[1], GROUP, 2))
    both = jnp.concatenate([first, packed[2]], axis=1).astype(jnp.bfloat16)
    out_ref[:, 0] = both
    out_ref[:, 1] = both


def join_and_mix(pieces_ref, matrix_ref, out_ref):
    lane = lax.broadcasted_iota(jnp.int32, (8, LANES), 1)
    rows = []
    for block in range(4):
        tiles = [[None] * (UNITS // LANES) for _ in range(3)]
        for group in range(GROUPS):
            piece = pieces_ref[block * GROUPS + group].astype(jnp.float32)
            start = GROUP * group
            tile, offset = start // LANES, start % LANES
            for row, (source, shift) in enumerate(((0, 0), (0, GROUP), (1, 0))):
                moved = piece[source * 8 : source * 8 + 8]
                turn = (offset - shift) % LANES
                if turn:
                    moved = pltpu.roll(moved, turn, 1)
                line = tiles[row]
                line[tile] = moved if line[tile] is None else jnp.where(lane < offset, line[tile], moved)
                if offset + GROUP > LANES:
                    line[tile + 1] = moved
        rows += [jnp.concatenate(line, axis=1) for line in tiles]
    units = jnp.concatenate(rows, axis=0).astype(jnp.bfloat16)
    mixed = jnp.dot(units, matrix_ref[...], preferred_element_type=jnp.float32).astype(jnp.bfloat16)
    for copy in range(out_ref.shape[0]):
        out_ref[copy] = mixed


def per_device(drafts, gate_codes, gate_scales, up_codes, up_scales, down_codes, down_scales):
    core = lax.axis_index("c")
    depth = drafts.shape[1]
    rows = drafts.shape[0] * N_T
    half = rows // 2
    width = 2 * UNITS
    everyone = ("z", "yl", "yh")
    copies = call(
        copy_out,
        "copy_out",
        (N_T,) + drafts.shape,
        (drafts,),
        1_000,
        memory=pltpu.HBM,
        scratch=[pltpu.VMEM((8,) + drafts.shape, drafts.dtype), pltpu.SemaphoreType.DMA((N_T // 8,))],
    )
    gathered = lax.all_to_all(copies, ("z", "yl"), 0, 0, tiled=True).reshape(rows, depth)
    weights = call(
        dequantize_pair,
        "dequantize_pair",
        (depth, width),
        (gate_codes, gate_scales, up_codes, up_scales),
        3_000_000,
    )
    other_weights = lax.ppermute(weights, "c", CORES)
    flops = 2 * half * depth * width
    theirs = call(take_theirs, "take_theirs", (half, depth), (gathered,), 1_000)
    other_rows = lax.ppermute(theirs, "c", CORES)
    part, other_weights = call(
        times_own,
        "times_own",
        [((half, width), jnp.float32), ((depth, width), jnp.bfloat16)],
        (theirs, gathered, weights, other_weights),
        flops,
        specs=[pl.ANY, pltpu.VMEM, pltpu.VMEM, pltpu.HBM],
        scratch=[pltpu.SemaphoreType.DMA((4,))],
    )
    sums = call(add_other, "add_other", (half, width), (part, other_rows, other_weights), flops)
    sums = lax.all_to_all(sums.reshape(4, half // 4, width), "x", 0, 0, tiled=True)
    pieces = call(sum_and_cut, "sum_and_cut", (4 * GROUPS, 24, LANES), (sums,), 1_000_000)
    pieces = lax.all_to_all(pieces, everyone, 0, 0, tiled=True)
    pieces = call(
        gate_and_mix, "gate_and_mix", (N_T, 2, 16, LANES), (pieces.reshape(N_T, 2, 24, LANES),), 2_000_000
    )
    pieces = lax.all_to_all(pieces.reshape(2 * N_T, 16, LANES), everyone, 0, 0, tiled=True)
    rotated = call(
        join_and_mix, "join_and_mix", (4, half // 4, UNITS), (pieces, jnp.asarray(block_matrix())), 200_000_000
    )
    rotated = lax.all_to_all(rotated, "x", 0, 0, tiled=True).reshape(half, UNITS)
    other = lax.ppermute(rotated, "c", CORES)
    down_weights = dequantize(down_codes, down_scales)
    own_part = jnp.dot(rotated, down_weights, preferred_element_type=jnp.float32)
    other_part = jnp.dot(other, down_weights, preferred_element_type=jnp.float32)
    own_part, other_part = own_part.astype(jnp.bfloat16), other_part.astype(jnp.bfloat16)
    partial_value = jnp.zeros((rows, own_part.shape[1]), jnp.bfloat16)
    partial_value = lax.dynamic_update_slice_in_dim(partial_value, own_part, core * half, 0)
    partial_value = lax.dynamic_update_slice_in_dim(partial_value, other_part, (1 - core) * half, 0)
    partial_value = lax.all_to_all(
        partial_value.reshape(N_T, rows // N_T, own_part.shape[1]), ("z", "yl"), 0, 0, tiled=True
    )
    return jnp.sum(partial_value.astype(jnp.float32), axis=0).astype(jnp.bfloat16)


def solution(mesh):
    fine = Mesh(mesh.devices.reshape(2, 4, 2, 8, 4), ("yh", "x", "c", "z", "yl"))
    dp, tensor = ("yh", "x", "c"), ("z", "yl")
    return jax.shard_map(
        per_device,
        mesh=fine,
        in_specs=(
            P(tensor, dp),
            P(dp, tensor),
            P(dp, tensor),
            P(dp, tensor),
            P(dp, tensor),
            P(tensor, dp),
            P(tensor, dp),
        ),
        out_specs=P(tensor, dp),
        check_vma=False,
    )
```

```python
import math

import jax
import jax.numpy as jnp
import ml_dtypes
import numpy as np
from jax import lax
from jax.experimental import pallas as pl
from jax.experimental.pallas import tpu as pltpu
from jax.sharding import Mesh
from jax.sharding import PartitionSpec as P

HK = 28
HB = 1024
G = 128
N_T = 32
SPAN = HB // N_T
UNITS = SPAN * HK
GROUP = 56
GROUPS = UNITS // GROUP
LANES = 128
CORES = [(0, 1), (1, 0)]
SCALE = 1.0 / math.sqrt(HK * HB)


def paley_matrix():
    modulus = 13
    residues = set((number * number % modulus for number in range(1, modulus)))
    character = np.array([0] + [1 if number in residues else -1 for number in range(1, modulus)])
    jacobsthal = character[(np.arange(modulus)[:, None] - np.arange(modulus)[None, :]) % modulus]
    top_row = np.concatenate([np.zeros((1, 1)), np.ones((1, modulus))], axis=1)
    lower_rows = np.concatenate([np.ones((modulus, 1)), jacobsthal], axis=1)
    conference = np.concatenate([top_row, lower_rows], axis=0)
    first_part = np.kron(conference, np.array([[1.0, -1.0], [-1.0, -1.0]]))
    second_part = np.kron(np.eye(modulus + 1), np.array([[1.0, 1.0], [1.0, -1.0]]))
    return first_part + second_part


def walsh(extent):
    matrix = np.ones((1, 1))
    while matrix.shape[0] < extent:
        matrix = np.kron(np.array([[1.0, 1.0], [1.0, -1.0]]), matrix)
    return matrix


def block_matrix():
    return np.kron(walsh(SPAN), paley_matrix()).T.astype(ml_dtypes.bfloat16)


def dequantize(codes, scales):
    row_count, col_count = codes.shape
    grouped = (
        codes.astype(jnp.float32).reshape(row_count // G, G, col_count) * scales[:, None, :]
    )
    return grouped.reshape(row_count, col_count).astype(jnp.bfloat16)


def whole(memory=pltpu.VMEM):
    return pl.BlockSpec(memory_space=memory)


def call(kernel, name, out_shape, operands, flops, memory=pltpu.VMEM, scratch=(), specs=None):
    places = specs or [pltpu.VMEM] * len(operands)
    if isinstance(out_shape, list):
        shapes = [jax.ShapeDtypeStruct(shape, dtype) for shape, dtype in out_shape]
        results = [whole(memory)] * len(shapes)
    else:
        shapes, results = jax.ShapeDtypeStruct(out_shape, jnp.bfloat16), whole(memory)
    return pl.pallas_call(
        kernel,
        out_shape=shapes,
        in_specs=[whole(place) for place in places],
        out_specs=results,
        scratch_shapes=list(scratch),
        name=name,
        compiler_params=pltpu.CompilerParams(vmem_limit_bytes=32 * 1024 * 1024),
        cost_estimate=pl.CostEstimate(flops=flops, bytes_accessed=2_000_000, transcendentals=0),
    )(*operands)


def copy_out(block_ref, out_ref, held, sems):
    at_once = held.shape[0]
    for index in range(at_once):
        held[index] = block_ref[...]
    copies = [
        pltpu.make_async_copy(held, out_ref.at[pl.ds(at_once * index, at_once)], sems.at[index])
        for index in range(out_ref.shape[0] // at_once)
    ]
    for copy in copies:
        copy.start()
    for copy in copies:
        copy.wait()


def dequantize_pair(gate_ref, gate_scales_ref, up_ref, up_scales_ref, out_ref):
    for group in range(gate_scales_ref.shape[0]):
        rows = pl.ds(group * G, G)
        line = slice(group, group + 1)
        gate = gate_ref[rows, :].astype(jnp.float32) * gate_scales_ref[line, :]
        up = up_ref[rows, :].astype(jnp.float32) * up_scales_ref[line, :]
        out_ref[rows, :UNITS] = gate.astype(jnp.bfloat16)
        out_ref[rows, UNITS:] = up.astype(jnp.bfloat16)


def dequantize_one(codes_ref, scales_ref, out_ref):
    for group in range(scales_ref.shape[0]):
        rows = pl.ds(group * G, G)
        weights = codes_ref[rows, :].astype(jnp.float32) * scales_ref[group : group + 1, :]
        out_ref[rows, :] = weights.astype(jnp.bfloat16)


def take_theirs(after_ref, rows_ref, out_ref):
    half = out_ref.shape[0]
    start = (1 - lax.axis_index("c")) * half
    out_ref[...] = rows_ref[pl.ds(pl.multiple_of(start, half), half), :]


def fetch(source_ref, target_ref, sems):
    step = source_ref.shape[0] // sems.shape[0]
    copies = []
    for index in range(sems.shape[0]):
        lines = pl.ds(index * step, step)
        copies.append(pltpu.make_async_copy(source_ref.at[lines], target_ref.at[lines], sems.at[index]))
        copies[-1].start()
    return copies


def times_own(after_ref, rows_ref, weights_ref, other_ref, out_ref, held_ref, sems):
    copies = fetch(other_ref, held_ref, sems)
    half = out_ref.shape[0]
    start = lax.axis_index("c") * half
    rows = rows_ref[pl.ds(pl.multiple_of(start, half), half), :]
    out_ref[...] = jnp.dot(rows, weights_ref[...], preferred_element_type=jnp.float32)
    for copy in copies:
        copy.wait()


def add_other(part_ref, rows_ref, weights_ref, out_ref):
    total = part_ref[...] + jnp.dot(rows_ref[...], weights_ref[...], preferred_element_type=jnp.float32)
    out_ref[...] = total.astype(jnp.bfloat16)


def times_down(after_ref, rows_ref, weights_ref, out_ref):
    total = jnp.dot(rows_ref[...], weights_ref[...], preferred_element_type=jnp.float32)
    out_ref[...] = total.astype(jnp.bfloat16)


def place_halves(own_ref, other_ref, out_ref):
    half = own_ref.shape[0]
    core = lax.axis_index("c")
    out_ref[pl.ds(pl.multiple_of(core * half, half), half), :] = own_ref[...]
    out_ref[pl.ds(pl.multiple_of((1 - core) * half, half), half), :] = other_ref[...]


def sum_and_cut(parts_ref, out_ref):
    total = parts_ref[0].astype(jnp.float32)
    for part in range(1, parts_ref.shape[0]):
        total = total + parts_ref[part].astype(jnp.float32)
    lane = lax.broadcasted_iota(jnp.int32, (total.shape[0], LANES), 1)
    for group in range(GROUPS):
        offset = GROUP * group % LANES
        halves = []
        for base, shift in ((0, 0), (UNITS, GROUP)):
            tile = (base + GROUP * group) // LANES * LANES
            piece = total[:, tile : tile + LANES]
            if offset + GROUP > LANES:
                piece = jnp.where(lane < offset, total[:, tile + LANES : tile + 2 * LANES], piece)
            turn = (shift - offset) % LANES
            halves.append(pltpu.roll(piece, turn, 1) if turn else piece)
        piece = jnp.where(lane < GROUP, halves[0], halves[1]).astype(jnp.bfloat16)
        for rows in range(4):
            out_ref[rows * GROUPS + group] = piece[rows * 24 : rows * 24 + 24]


def gate_and_mix(sums_ref, out_ref):
    sums = sums_ref[:, 0].astype(jnp.float32) + sums_ref[:, 1].astype(jnp.float32)
    lane = lax.broadcasted_iota(jnp.int32, (N_T, 8, LANES), 2)
    packed = []
    for tile in range(3):
        gate = sums[:, tile * 8 : tile * 8 + 8]
        up = pltpu.roll(gate, LANES - GROUP, 2)
        value = (gate / (1.0 + jnp.exp(-gate)) * up).astype(jnp.bfloat16).astype(jnp.float32)
        value = jnp.where(lane < GROUP, value, 0.0)
        half = 1
        while half < N_T:
            split = value.reshape(N_T // (2 * half), 2, half, 8, LANES)
            low, high = split[:, 0], split[:, 1]
            value = jnp.stack([low + high, low - high], axis=1).reshape(N_T, 8, LANES)
            half *= 2
        packed.append(value * SCALE)
    first = jnp.where(lane < GROUP, packed[0], pltpu.roll(packed[1], GROUP, 2))
    both = jnp.concatenate([first, packed[2]], axis=1).astype(jnp.bfloat16)
    out_ref[:, 0] = both
    out_ref[:, 1] = both


def join_and_mix(pieces_ref, matrix_ref, out_ref):
    lane = lax.broadcasted_iota(jnp.int32, (8, LANES), 1)
    rows = []
    for block in range(4):
        tiles = [[None] * (UNITS // LANES) for _ in range(3)]
        for group in range(GROUPS):
            piece = pieces_ref[block * GROUPS + group].astype(jnp.float32)
            start = GROUP * group
            tile, offset = start // LANES, start % LANES
            for row, (source, shift) in enumerate(((0, 0), (0, GROUP), (1, 0))):
                moved = piece[source * 8 : source * 8 + 8]
                turn = (offset - shift) % LANES
                if turn:
                    moved = pltpu.roll(moved, turn, 1)
                line = tiles[row]
                line[tile] = moved if line[tile] is None else jnp.where(lane < offset, line[tile], moved)
                if offset + GROUP > LANES:
                    line[tile + 1] = moved
        rows += [jnp.concatenate(line, axis=1) for line in tiles]
    units = jnp.concatenate(rows, axis=0).astype(jnp.bfloat16)
    mixed = jnp.dot(units, matrix_ref[...], preferred_element_type=jnp.float32).astype(jnp.bfloat16)
    for copy in range(out_ref.shape[0]):
        out_ref[copy] = mixed


def per_device(drafts, gate_codes, gate_scales, up_codes, up_scales, down_codes, down_scales):
    core = lax.axis_index("c")
    depth = drafts.shape[1]
    rows = drafts.shape[0] * N_T
    half = rows // 2
    width = 2 * UNITS
    everyone = ("z", "yl", "yh")
    copies = call(
        copy_out,
        "copy_out",
        (N_T,) + drafts.shape,
        (drafts,),
        1_000,
        memory=pltpu.HBM,
        scratch=[pltpu.VMEM((8,) + drafts.shape, drafts.dtype), pltpu.SemaphoreType.DMA((N_T // 8,))],
    )
    gathered = lax.all_to_all(copies, ("z", "yl"), 0, 0, tiled=True).reshape(rows, depth)
    columns = down_codes.shape[1]
    weights = call(
        dequantize_pair,
        "dequantize_pair",
        (depth, width),
        (gate_codes, gate_scales, up_codes, up_scales),
        3_000_000,
    )
    other_weights = lax.ppermute(weights, "c", CORES)
    down = call(dequantize_one, "dequantize_one", down_codes.shape, (down_codes, down_scales), 1_000_000)
    other_down = lax.ppermute(down, "c", CORES)
    flops = 2 * half * depth * width
    theirs = call(take_theirs, "take_theirs", (half, depth), (other_down[:16, :LANES], gathered), 1_000)
    other_rows = lax.ppermute(theirs, "c", CORES)
    part, other_pair = call(
        times_own,
        "times_own",
        [((half, width), jnp.float32), ((depth, width), jnp.bfloat16)],
        (theirs, gathered, weights, other_weights),
        flops,
        specs=[pl.ANY, pltpu.VMEM, pltpu.VMEM, pltpu.HBM],
        scratch=[pltpu.SemaphoreType.DMA((4,))],
    )
    sums = call(add_other, "add_other", (half, width), (part, other_rows, other_pair), flops)
    sums = lax.all_to_all(sums.reshape(4, half // 4, width), "x", 0, 0, tiled=True)
    pieces = call(sum_and_cut, "sum_and_cut", (4 * GROUPS, 24, LANES), (sums,), 1_000_000)
    pieces = lax.all_to_all(pieces, everyone, 0, 0, tiled=True)
    pieces = call(
        gate_and_mix, "gate_and_mix", (N_T, 2, 16, LANES), (pieces.reshape(N_T, 2, 24, LANES),), 2_000_000
    )
    pieces = lax.all_to_all(pieces.reshape(2 * N_T, 16, LANES), everyone, 0, 0, tiled=True)
    rotated = call(
        join_and_mix, "join_and_mix", (4, half // 4, UNITS), (pieces, jnp.asarray(block_matrix())), 200_000_000
    )
    rotated = lax.all_to_all(rotated, "x", 0, 0, tiled=True).reshape(half, UNITS)
    flops = 2 * half * UNITS * columns
    places = [pl.ANY, pltpu.VMEM, pltpu.VMEM]
    sent = call(
        times_down,
        "their_columns",
        (half, columns),
        (rotated, rotated, other_down),
        flops,
        specs=places,
    )
    received = lax.ppermute(sent, "c", CORES)
    kept = call(
        times_down,
        "our_columns",
        (half, columns),
        (sent, rotated, down),
        flops,
        specs=places,
    )
    partial_value = call(place_halves, "place_halves", (rows, columns), (kept, received), 1_000)
    partial_value = lax.all_to_all(
        partial_value.reshape(N_T, rows // N_T, columns), ("z", "yl"), 0, 0, tiled=True
    )
    return jnp.sum(partial_value.astype(jnp.float32), axis=0).astype(jnp.bfloat16)


def solution(mesh):
    fine = Mesh(mesh.devices.reshape(2, 4, 2, 8, 4), ("yh", "x", "c", "z", "yl"))
    dp, tensor = ("yh", "x", "c"), ("z", "yl")
    return jax.shard_map(
        per_device,
        mesh=fine,
        in_specs=(
            P(tensor, dp),
            P(dp, tensor),
            P(dp, tensor),
            P(dp, tensor),
            P(dp, tensor),
            P(tensor, dp),
            P(tensor, dp),
        ),
        out_specs=P(tensor, dp),
        check_vma=False,
    )
```

```python
import math

import jax
import jax.numpy as jnp
import ml_dtypes
import numpy as np
from jax import lax
from jax.experimental import pallas as pl
from jax.experimental.pallas import tpu as pltpu
from jax.sharding import Mesh
from jax.sharding import PartitionSpec as P

HK = 28
HB = 1024
G = 128
N_T = 32
SPAN = HB // N_T
UNITS = SPAN * HK
GROUP = 56
GROUPS = UNITS // GROUP
LANES = 128
CORES = [(0, 1), (1, 0)]
SCALE = 1.0 / math.sqrt(HK * HB)


def paley_matrix():
    modulus = 13
    residues = set((number * number % modulus for number in range(1, modulus)))
    character = np.array([0] + [1 if number in residues else -1 for number in range(1, modulus)])
    jacobsthal = character[(np.arange(modulus)[:, None] - np.arange(modulus)[None, :]) % modulus]
    top_row = np.concatenate([np.zeros((1, 1)), np.ones((1, modulus))], axis=1)
    lower_rows = np.concatenate([np.ones((modulus, 1)), jacobsthal], axis=1)
    conference = np.concatenate([top_row, lower_rows], axis=0)
    first_part = np.kron(conference, np.array([[1.0, -1.0], [-1.0, -1.0]]))
    second_part = np.kron(np.eye(modulus + 1), np.array([[1.0, 1.0], [1.0, -1.0]]))
    return first_part + second_part


def walsh(extent):
    matrix = np.ones((1, 1))
    while matrix.shape[0] < extent:
        matrix = np.kron(np.array([[1.0, 1.0], [1.0, -1.0]]), matrix)
    return matrix


def block_matrix():
    return np.kron(walsh(SPAN), paley_matrix()).T.astype(ml_dtypes.bfloat16)


def dequantize(codes, scales):
    row_count, col_count = codes.shape
    grouped = (
        codes.astype(jnp.float32).reshape(row_count // G, G, col_count) * scales[:, None, :]
    )
    return grouped.reshape(row_count, col_count).astype(jnp.bfloat16)


def whole(memory=pltpu.VMEM):
    return pl.BlockSpec(memory_space=memory)


def call(kernel, name, out_shape, operands, flops, memory=pltpu.VMEM, scratch=(), specs=None):
    places = specs or [pltpu.VMEM] * len(operands)
    if isinstance(out_shape, list):
        shapes = [jax.ShapeDtypeStruct(shape, dtype) for shape, dtype in out_shape]
        results = [whole(memory)] * len(shapes)
    else:
        shapes, results = jax.ShapeDtypeStruct(out_shape, jnp.bfloat16), whole(memory)
    return pl.pallas_call(
        kernel,
        out_shape=shapes,
        in_specs=[whole(place) for place in places],
        out_specs=results,
        scratch_shapes=list(scratch),
        name=name,
        compiler_params=pltpu.CompilerParams(vmem_limit_bytes=32 * 1024 * 1024),
        cost_estimate=pl.CostEstimate(flops=flops, bytes_accessed=2_000_000, transcendentals=0),
    )(*operands)


def copy_out(block_ref, out_ref, held, sems):
    at_once = held.shape[0]
    for index in range(at_once):
        held[index] = block_ref[...]
    copies = [
        pltpu.make_async_copy(held, out_ref.at[pl.ds(at_once * index, at_once)], sems.at[index])
        for index in range(out_ref.shape[0] // at_once)
    ]
    for copy in copies:
        copy.start()
    for copy in copies:
        copy.wait()


def dequantize_pair(gate_ref, gate_scales_ref, up_ref, up_scales_ref, out_ref):
    for group in range(gate_scales_ref.shape[0]):
        rows = pl.ds(group * G, G)
        line = slice(group, group + 1)
        gate = gate_ref[rows, :].astype(jnp.float32) * gate_scales_ref[line, :]
        up = up_ref[rows, :].astype(jnp.float32) * up_scales_ref[line, :]
        out_ref[rows, :UNITS] = gate.astype(jnp.bfloat16)
        out_ref[rows, UNITS:] = up.astype(jnp.bfloat16)


def dequantize_one(codes_ref, scales_ref, out_ref):
    for group in range(scales_ref.shape[0]):
        rows = pl.ds(group * G, G)
        weights = codes_ref[rows, :].astype(jnp.float32) * scales_ref[group : group + 1, :]
        out_ref[rows, :] = weights.astype(jnp.bfloat16)


def take_theirs(after_ref, rows_ref, out_ref):
    half = out_ref.shape[0]
    start = (1 - lax.axis_index("c")) * half
    out_ref[...] = rows_ref[pl.ds(pl.multiple_of(start, half), half), :]


def fetch(source_ref, target_ref, sems):
    step = source_ref.shape[0] // sems.shape[0]
    copies = []
    for index in range(sems.shape[0]):
        lines = pl.ds(index * step, step)
        copies.append(pltpu.make_async_copy(source_ref.at[lines], target_ref.at[lines], sems.at[index]))
        copies[-1].start()
    return copies


def times_own(after_ref, rows_ref, weights_ref, other_ref, out_ref, held_ref, sems):
    copies = fetch(other_ref, held_ref, sems)
    half = out_ref.shape[0]
    start = lax.axis_index("c") * half
    rows = rows_ref[pl.ds(pl.multiple_of(start, half), half), :]
    out_ref[...] = jnp.dot(rows, weights_ref[...], preferred_element_type=jnp.float32)
    for copy in copies:
        copy.wait()


def add_other(part_ref, rows_ref, weights_ref, out_ref):
    total = part_ref[...] + jnp.dot(rows_ref[...], weights_ref[...], preferred_element_type=jnp.float32)
    out_ref[...] = total.astype(jnp.bfloat16)


def times_down(after_ref, rows_ref, weights_ref, out_ref):
    total = jnp.dot(rows_ref[...], weights_ref[...], preferred_element_type=jnp.float32)
    out_ref[...] = total.astype(jnp.bfloat16)


def place_halves(own_ref, other_ref, out_ref):
    half = own_ref.shape[0]
    core = lax.axis_index("c")
    out_ref[pl.ds(pl.multiple_of(core * half, half), half), :] = own_ref[...]
    out_ref[pl.ds(pl.multiple_of((1 - core) * half, half), half), :] = other_ref[...]


def sum_and_cut(parts_ref, out_ref):
    total = parts_ref[0].astype(jnp.float32)
    for part in range(1, parts_ref.shape[0]):
        total = total + parts_ref[part].astype(jnp.float32)
    lane = lax.broadcasted_iota(jnp.int32, (total.shape[0], LANES), 1)
    for group in range(GROUPS):
        offset = GROUP * group % LANES
        halves = []
        for base, shift in ((0, 0), (UNITS, GROUP)):
            tile = (base + GROUP * group) // LANES * LANES
            piece = total[:, tile : tile + LANES]
            if offset + GROUP > LANES:
                piece = jnp.where(lane < offset, total[:, tile + LANES : tile + 2 * LANES], piece)
            turn = (shift - offset) % LANES
            halves.append(pltpu.roll(piece, turn, 1) if turn else piece)
        piece = jnp.where(lane < GROUP, halves[0], halves[1]).astype(jnp.bfloat16)
        for rows in range(4):
            out_ref[rows * GROUPS + group] = piece[rows * 24 : rows * 24 + 24]


def gate_and_mix(sums_ref, out_ref):
    sums = sums_ref[:, 0].astype(jnp.float32) + sums_ref[:, 1].astype(jnp.float32)
    lane = lax.broadcasted_iota(jnp.int32, (N_T, 8, LANES), 2)
    packed = []
    for tile in range(3):
        gate = sums[:, tile * 8 : tile * 8 + 8]
        up = pltpu.roll(gate, LANES - GROUP, 2)
        value = (gate / (1.0 + jnp.exp(-gate)) * up).astype(jnp.bfloat16).astype(jnp.float32)
        value = jnp.where(lane < GROUP, value, 0.0)
        half = 1
        while half < N_T:
            split = value.reshape(N_T // (2 * half), 2, half, 8, LANES)
            low, high = split[:, 0], split[:, 1]
            value = jnp.stack([low + high, low - high], axis=1).reshape(N_T, 8, LANES)
            half *= 2
        packed.append(value * SCALE)
    first = jnp.where(lane < GROUP, packed[0], pltpu.roll(packed[1], GROUP, 2))
    both = jnp.concatenate([first, packed[2]], axis=1).astype(jnp.bfloat16)
    out_ref[:, 0] = both
    out_ref[:, 1] = both


def join_and_mix(pieces_ref, matrix_ref, out_ref):
    lane = lax.broadcasted_iota(jnp.int32, (8, LANES), 1)
    rows = []
    for block in range(4):
        tiles = [[None] * (UNITS // LANES) for _ in range(3)]
        for group in range(GROUPS):
            piece = pieces_ref[block * GROUPS + group].astype(jnp.float32)
            start = GROUP * group
            tile, offset = start // LANES, start % LANES
            for row, (source, shift) in enumerate(((0, 0), (0, GROUP), (1, 0))):
                moved = piece[source * 8 : source * 8 + 8]
                turn = (offset - shift) % LANES
                if turn:
                    moved = pltpu.roll(moved, turn, 1)
                line = tiles[row]
                line[tile] = moved if line[tile] is None else jnp.where(lane < offset, line[tile], moved)
                if offset + GROUP > LANES:
                    line[tile + 1] = moved
        rows += [jnp.concatenate(line, axis=1) for line in tiles]
    units = jnp.concatenate(rows, axis=0).astype(jnp.bfloat16)
    mixed = jnp.dot(units, matrix_ref[...], preferred_element_type=jnp.float32).astype(jnp.bfloat16)
    for copy in range(out_ref.shape[0]):
        out_ref[copy] = mixed


def per_device(drafts, gate_codes, gate_scales, up_codes, up_scales, down_codes, down_scales):
    core = lax.axis_index("c")
    depth = drafts.shape[1]
    rows = drafts.shape[0] * N_T
    half = rows // 2
    width = 2 * UNITS
    everyone = ("z", "yl", "yh")
    copies = call(
        copy_out,
        "copy_out",
        (N_T,) + drafts.shape,
        (drafts,),
        1_000,
        memory=pltpu.HBM,
        scratch=[pltpu.VMEM((8,) + drafts.shape, drafts.dtype), pltpu.SemaphoreType.DMA((N_T // 8,))],
    )
    gathered = lax.all_to_all(copies, ("z", "yl"), 0, 0, tiled=True).reshape(rows, depth)
    columns = down_codes.shape[1]
    weights = call(
        dequantize_pair,
        "dequantize_pair",
        (depth, width),
        (gate_codes, gate_scales, up_codes, up_scales),
        3_000_000,
    )
    other_weights = lax.ppermute(weights, "c", CORES)
    down = call(dequantize_one, "dequantize_one", down_codes.shape, (down_codes, down_scales), 1_000_000)
    other_down = lax.ppermute(down, "c", CORES)
    flops = 2 * half * depth * width
    theirs = call(take_theirs, "take_theirs", (half, depth), (other_down[:16, :LANES], gathered), 1_000)
    other_rows = lax.ppermute(theirs, "c", CORES)
    part, other_pair = call(
        times_own,
        "times_own",
        [((half, width), jnp.float32), ((depth, width), jnp.bfloat16)],
        (theirs, gathered, weights, other_weights),
        flops,
        specs=[pl.ANY, pltpu.VMEM, pltpu.VMEM, pltpu.HBM],
        scratch=[pltpu.SemaphoreType.DMA((16,))],
    )
    sums = call(add_other, "add_other", (half, width), (part, other_rows, other_pair), flops)
    sums = lax.all_to_all(sums.reshape(4, half // 4, width), "x", 0, 0, tiled=True)
    pieces = call(sum_and_cut, "sum_and_cut", (4 * GROUPS, 24, LANES), (sums,), 1_000_000)
    pieces = lax.all_to_all(pieces, everyone, 0, 0, tiled=True)
    pieces = call(
        gate_and_mix, "gate_and_mix", (N_T, 2, 16, LANES), (pieces.reshape(N_T, 2, 24, LANES),), 2_000_000
    )
    pieces = lax.all_to_all(pieces.reshape(2 * N_T, 16, LANES), everyone, 0, 0, tiled=True)
    rotated = call(
        join_and_mix, "join_and_mix", (4, half // 4, UNITS), (pieces, jnp.asarray(block_matrix())), 200_000_000
    )
    rotated = lax.all_to_all(rotated, "x", 0, 0, tiled=True).reshape(half, UNITS)
    flops = 2 * half * UNITS * columns
    places = [pl.ANY, pltpu.VMEM, pltpu.VMEM]
    sent = call(
        times_down,
        "their_columns",
        (half, columns),
        (rotated, rotated, other_down),
        flops,
        specs=places,
    )
    received = lax.ppermute(sent, "c", CORES)
    kept = call(
        times_down,
        "our_columns",
        (half, columns),
        (sent, rotated, down),
        flops,
        specs=places,
    )
    partial_value = call(place_halves, "place_halves", (rows, columns), (kept, received), 1_000)
    partial_value = lax.all_to_all(
        partial_value.reshape(N_T, rows // N_T, columns), ("z", "yl"), 0, 0, tiled=True
    )
    return jnp.sum(partial_value.astype(jnp.float32), axis=0).astype(jnp.bfloat16)


def solution(mesh):
    fine = Mesh(mesh.devices.reshape(2, 4, 2, 8, 4), ("yh", "x", "c", "z", "yl"))
    dp, tensor = ("yh", "x", "c"), ("z", "yl")
    return jax.shard_map(
        per_device,
        mesh=fine,
        in_specs=(
            P(tensor, dp),
            P(dp, tensor),
            P(dp, tensor),
            P(dp, tensor),
            P(dp, tensor),
            P(tensor, dp),
            P(tensor, dp),
        ),
        out_specs=P(tensor, dp),
        check_vma=False,
    )
```
